256 devices in a mesh: slab: 64 (over z, y, core), grp: 4 (over x).
Axes of the slice: x: 4, y: 4, z: 8, core: 2. Of those that a mesh axis runs over, the one named last changes fastest.
Arguments:
- positions: float32 [256, 3, 8192], P(('slab', 'grp')), may hold values from 0 to 1
- masses: float32 [256, 8192], P(('slab', 'grp')), may hold values from 0.001 to 0.01
- smoothing: float32 [256, 8192], P(('slab', 'grp')), may hold values from 0.3 to 0.6
- block_lists: int32 [256, 64, 8], P(('slab', 'grp')), may hold values from 0 to 63, as said below
- block_counts: int32 [256, 64], P(('slab', 'grp')), may hold values from 0 to 128, as said below
- group_owner: int32 [4, 64], P('grp'), may hold values from 0 to 63, each once within a row
Outputs:
- density: float32 [256, 8192], P(('slab', 'grp'))
- potential: float32 [256, 8192], P(('slab', 'grp'))
- group_energy: float32 [4, 64], P('grp', 'slab')
The draws below stay inside these ranges and needn't reach their ends.
Inputs may be any that keep to these rules, and one draw needn't show every extreme that they name: `block_lists`: columns 0 to 1 name blocks of the slab below, the next 4 columns blocks of the own slab, the first of them the block itself, and the last 2 columns blocks of the slab above; the entries of each of these three sets differ. Block c of a slab lists block b of the slab below in its first 2 columns exactly when block b lists block c in its last 2 columns. `block_counts`: within one subgroup, a slab's rows begin with the members of its groups, group after group in order of group number. In every subgroup one group has 128 members on every slab.
All inputs are finite; a program needn't handle non-finite values.
Results may differ from the reference program's by a relative error of at most 0.0003.
Values sent between devices are 32-bit elements; how exact they have to be, the bound alone decides.
No kernel may reach another device: no remote copies, remote signals or barrier semaphores. Data moves between devices by JAX's collectives and lax.ppermute only.
A program may use at most 64 MiB of HBM per device.

```python
import math
import jax
import jax.numpy as jnp
from jax import lax

TILE = 128
PB = 64
KX = 2
KO = 4
PARTS_DEV = 8192
NSP = 256
GROUPS = 64
N_SLAB = 64
N_GRP = 4


def draw_block_lists(key, part):
    cross_key = jax.random.fold_in(key, 11)
    own_key = jax.random.fold_in(key, 12)

    def permute_cross(sub_key):
        return jax.random.permutation(sub_key, PB)

    def permute_own(sub_key):
        return jax.random.permutation(sub_key, PB - 1)
    crossing = jax.vmap(permute_cross)(jax.random.split(cross_key, NSP)).astype(jnp.int32)
    inverse = jnp.argsort(crossing, axis=1).astype(jnp.int32)
    block_ids = jnp.arange(PB, dtype=jnp.int32)
    steps = jnp.arange(KX, dtype=jnp.int32)
    upward = crossing[:, (block_ids[:, None] + steps[None, :]) % PB]
    previous = jnp.roll(inverse, 1, axis=0)
    downward = (previous[:, :, None] - steps[None, None, :]) % PB
    offsets = jax.vmap(permute_own)(jax.random.split(own_key, NSP * PB)).astype(jnp.int32)
    offsets = offsets[:, :KO - 1].reshape(NSP, PB, KO - 1) + 1
    own_self = jnp.broadcast_to(block_ids[None, :, None], (NSP, PB, 1))
    own_other = (block_ids[None, :, None] + offsets) % PB
    return jnp.concatenate([downward, own_self, own_other, upward], axis=2).astype(jnp.int32)


def draw_block_counts(key, part):
    hottest = jax.random.randint(jax.random.fold_in(key, 21), (N_GRP,), 0, GROUPS)
    counts = jax.random.randint(jax.random.fold_in(key, 22), (NSP, GROUPS), 0, 2 * TILE // 3 + 1)
    subgroup = jnp.arange(NSP, dtype=jnp.int32) % N_GRP
    is_hot = jnp.arange(GROUPS, dtype=jnp.int32)[None, :] == hottest[subgroup][:, None]
    return jnp.where(is_hot, TILE, counts).astype(jnp.int32)


def level_of(key, shape, cuts, least, high):
    gain, own = 1.0, jax.random.fold_in(key, 6)
    for position, parts in cuts:
        heights = jnp.exp(jax.random.uniform(jax.random.fold_in(own, position), (parts,), jnp.float32, least / len(cuts), high / len(cuts)))
        gain = gain * jnp.repeat(heights, shape[position] // parts).reshape([-1 if axis == position else 1 for axis in range(len(shape))])
    return gain


def setup_inputs(seed: int = 0) -> dict:
    arg_keys = jax.random.split(jax.random.key(seed), 7)
    positions = jnp.clip(1.0 * jax.random.uniform(arg_keys[0], (NSP, 3, PARTS_DEV), jnp.float32) ** level_of(arg_keys[0], (NSP, 3, PARTS_DEV), ((0, 256),), -0.2, 0.2), 0.0, 1.0)
    masses = jnp.clip(jnp.exp(math.log(0.01) - 2.30258502 * jax.random.uniform(arg_keys[1], (NSP, PARTS_DEV), jnp.float32) ** level_of(arg_keys[1], (NSP, PARTS_DEV), ((0, 256),), -0.2, 0.2)), 0.001, 0.01)
    smoothing = jnp.clip(jnp.exp(math.log(0.6) - 0.6931472 * jax.random.uniform(arg_keys[2], (NSP, PARTS_DEV), jnp.float32) ** level_of(arg_keys[2], (NSP, PARTS_DEV), ((0, 256),), -0.2, 0.2)), 0.3, 0.6)
    block_lists = draw_block_lists(jax.random.fold_in(arg_keys[6], 71), 0)
    block_counts = draw_block_counts(jax.random.fold_in(arg_keys[6], 71), 0)
    group_owner = jax.vmap(lambda own: jax.random.permutation(own, N_SLAB))(jax.random.split(arg_keys[5], N_GRP)).reshape((N_GRP, GROUPS)).astype(jnp.int32)
    return {"positions": positions, "masses": masses, "smoothing": smoothing, "block_lists": block_lists, "block_counts": block_counts, "group_owner": group_owner}


KERNEL_NORM = 21.0 / (16.0 * math.pi)

def kernel_tile(target, source):
    delta_x = target[..., 0, :, None] - source[..., 0, None, :]
    delta_y = target[..., 1, :, None] - source[..., 1, None, :]
    delta_z = target[..., 2, :, None] - source[..., 2, None, :]
    pair_size = 0.5 * (target[..., 4, :, None] + source[..., 4, None, :])
    scaled = jnp.sqrt(delta_x * delta_x + delta_y * delta_y + delta_z * delta_z) / pair_size
    falloff = jnp.maximum(1.0 - 0.5 * scaled, 0.0)
    falloff_sq = falloff * falloff
    return KERNEL_NORM / (pair_size * pair_size * pair_size) * falloff_sq * falloff_sq * (1.0 + 2.0 * scaled)

def to_blocks(particles):
    return particles.reshape(5, PB, TILE).transpose(1, 0, 2)

def group_potential(members):
    total_rows = members.shape[1]
    width = min(512, total_rows)
    softness = 0.25 * members[4] * members[4]

    def row_block(start):
        target = lax.dynamic_slice_in_dim(members, start, width, 1)
        target_soft = lax.dynamic_slice_in_dim(softness, start, width, 0)
        delta_x = target[0][:, None] - members[0][None, :]
        delta_y = target[1][:, None] - members[1][None, :]
        delta_z = target[2][:, None] - members[2][None, :]
        inverse = lax.rsqrt(delta_x * delta_x + delta_y * delta_y + delta_z * delta_z + 0.5 * (target_soft[:, None] + softness[None, :]))
        summed = lax.optimization_barrier(jnp.sum(inverse * members[3][None, :], axis=1))
        return target[3] * lax.rsqrt(target_soft) - summed
    starts = jnp.arange(total_rows // width, dtype=jnp.int32) * width
    return lax.map(row_block, starts).reshape(total_rows)

def reference(positions, masses, smoothing, block_lists, block_counts, group_owner):
    particles = jnp.concatenate([positions, masses[:, None, :], smoothing[:, None, :]], axis=1)
    slabs = particles.shape[0]
    row_count = particles.shape[2]
    blocks = jax.vmap(to_blocks)(particles)
    offset_x = jnp.array([1.0, 0.0, 0.0, 0.0, 0.0], jnp.float32)[:, None]
    lower = jnp.roll(blocks, 1, axis=0) - offset_x
    upper = jnp.roll(blocks, -1, axis=0) + offset_x
    candidates = jnp.concatenate([lower, blocks, upper], axis=1)
    column_base = jnp.concatenate([jnp.zeros((KX,), jnp.int32), jnp.full((KO,), PB, jnp.int32), jnp.full((KX,), 2 * PB, jnp.int32)])

    def one_slab(pieces):
        slab_cands, own_blocks, slab_lists = pieces
        picked = slab_cands[(slab_lists + column_base[None, :]).astype(jnp.int32)]

        def one_block(couple):
            target, sources = couple
            flat_src = sources.transpose(1, 0, 2).reshape(5, -1)
            return lax.optimization_barrier(jnp.sum(kernel_tile(target, flat_src) * flat_src[3][None, :], axis=1))
        return lax.map(one_block, (own_blocks, picked))
    density = lax.map(one_slab, (candidates, blocks, block_lists)).reshape(slabs, row_count)
    offsets = (jnp.cumsum(block_counts, axis=1) - block_counts).astype(jnp.int32)
    slot = jnp.arange(TILE, dtype=jnp.int32)
    row_index = jnp.minimum(offsets[:, :, None] + slot[None, None, :], row_count - 1).astype(jnp.int32)
    live = slot[None, None, :] < block_counts[:, :, None]

    def pick_rows(slab_parts, slab_index):
        return jnp.take(slab_parts, slab_index.reshape(-1), axis=1)
    picked = jax.vmap(pick_rows)(particles, row_index).reshape(slabs, 5, GROUPS, TILE)
    masked = jnp.where(live, picked[:, 3], 0.0)
    picked = jnp.concatenate([picked[:, :3], masked[:, None], picked[:, 4:]], axis=1)
    by_group = picked.reshape(N_SLAB, N_GRP, 5, GROUPS, TILE).transpose(1, 3, 2, 0, 4)
    members = by_group.reshape(N_GRP * GROUPS, 5, N_SLAB * TILE)

    def one_group(group_rows):
        values = group_potential(group_rows)
        return (values, 0.5 * jnp.sum(group_rows[3] * values))
    potentials, energies = lax.map(one_group, members)
    returned = potentials.reshape(N_GRP, GROUPS, N_SLAB, TILE).transpose(2, 0, 1, 3)
    returned = returned.reshape(slabs, GROUPS * TILE)
    ends = (offsets + block_counts).astype(jnp.int32)
    all_rows = jnp.arange(row_count, dtype=jnp.int32)

    def one_map(pieces):
        slab_ends, slab_offsets, table = pieces
        member_of = lax.optimization_barrier(jnp.sum((slab_ends[None, :] <= all_rows[:, None]).astype(jnp.int32), axis=1)).astype(jnp.int32)
        bounded = jnp.minimum(member_of, GROUPS - 1)
        first_row = slab_offsets[bounded]
        flat_index = (bounded * TILE + jnp.clip(all_rows - first_row, 0, TILE - 1)).astype(jnp.int32)
        return jnp.where(member_of < GROUPS, table[flat_index], 0.0)
    potential = lax.map(one_map, (ends, offsets, returned))
    subgroup = jnp.arange(N_GRP, dtype=jnp.int32)[:, None]
    group_energy = jnp.zeros((N_GRP, N_SLAB), jnp.float32).at[subgroup, group_owner].set(energies.reshape(N_GRP, GROUPS))
    return (density, potential, group_energy)
```

```python
import functools
import math

import jax
import jax.numpy as jnp
from jax import lax
from jax.experimental import pallas as pl
from jax.experimental.pallas import tpu as pltpu
from jax.sharding import PartitionSpec as P

TILE = 128
PB = 64
KX = 2
KO = 4
COLS = 2 * KX + KO
GROUPS = 64
STEP = 512
PER_STEP = STEP // TILE
STEPS = PB // PER_STEP
KERNEL_NORM = 21.0 / (16.0 * math.pi)
VMEM = pl.BlockSpec(memory_space=pltpu.VMEM)
SMEM = pl.BlockSpec(memory_space=pltpu.SMEM)


def params():
    return pltpu.CompilerParams(vmem_limit_bytes=48 * 1024 * 1024)


def lanes(shape):
    return lax.broadcasted_iota(jnp.int32, shape, len(shape) - 1)


def rows(shape):
    return lax.broadcasted_iota(jnp.int32, shape, len(shape) - 2)


def factors(coords, extra):
    row = rows(coords.shape)
    high = coords.astype(jnp.bfloat16).astype(jnp.float32)
    low = coords - high
    norm = jnp.sum(coords * coords, axis=0, keepdims=True) + extra
    norm = jnp.broadcast_to(norm, coords.shape)
    n0 = norm.astype(jnp.bfloat16).astype(jnp.float32)
    rest = norm - n0
    n1 = rest.astype(jnp.bfloat16).astype(jnp.float32)
    n2 = rest - n1
    one = jnp.where(row < 6, 1.0, 0.0)
    lead = jnp.where(row == 0, n0, jnp.where(row == 1, n1, jnp.where(row == 2, n2, one)))
    tail = jnp.where(row == 3, n0, jnp.where(row == 4, n1, jnp.where(row == 5, n2, one)))
    target = jnp.concatenate([high, high, low, lead], axis=0)
    source = jnp.concatenate([-2.0 * high, -2.0 * low, -2.0 * high, tail], axis=0)
    return target, source


def pack_kernel(counts, owners, pos, mass, smooth, blocks, message):
    for c in range(PB):
        cut = slice(c * TILE, (c + 1) * TILE)
        blocks[c, 0:3, :] = pos[0, :, cut]
        blocks[c, 3:4, :] = mass[:, cut]
        blocks[c, 4:5, :] = smooth[:, cut]
        blocks[c, 5:8, :] = jnp.zeros((3, TILE), jnp.float32)
    lane = lanes((8, TILE))
    row = rows((8, TILE))

    def window(start):
        q = jnp.minimum(start // TILE, PB - 1)
        r = start % TILE
        both = jnp.where(lane >= r, blocks[q], blocks[jnp.minimum(q + 1, PB - 1)])
        return pltpu.roll(both, (TILE - r) % TILE, 1)

    def group(k, carry):
        start, hot, hot_start = carry
        count = counts[0, k]
        value = window(start)
        value = jnp.where((row == 3) & (lane >= count), 0.0, value)
        value = jnp.where(row == 5, count.astype(jnp.float32), value)
        message[owners[0, k], 0:8, :] = value
        first = (count == TILE) & (hot < 0)
        return (
            start + count,
            jnp.where(first, k, hot),
            jnp.where(first, start, hot_start),
        )

    _, hot, hot_start = lax.fori_loop(
        0, GROUPS, group, (jnp.int32(0), jnp.int32(-1), jnp.int32(0)), unroll=8
    )
    value = jnp.where(row == 5, hot.astype(jnp.float32), window(hot_start))
    for d in range(GROUPS):
        message[d, 8:16, :] = value


def density_kernel(lists, own, below, above, out, source, target, props, d_even, d_odd, wide_even, wide_odd):
    row = rows((8, TILE))

    def prepare(ref, base, shift, with_target):
        def step(c, _):
            block = ref[c]
            coords = jnp.where(row < 3, block - 0.5, 0.0)
            if shift:
                coords = jnp.where(row == 0, coords + shift, coords)
            f, g = factors(coords, 0.0)
            source[base + c] = g.astype(jnp.bfloat16)
            props[base + c] = block
            if with_target:
                target[c] = f.T.astype(jnp.bfloat16)
            return 0

        lax.fori_loop(0, PB, step, 0, unroll=4)

    prepare(below, 0, -1.0, False)
    prepare(own, PB, 0.0, True)
    prepare(above, 2 * PB, 1.0, False)

    def pick(b, s):
        base = 0 if s < KX else (PB if s < KX + KO else 2 * PB)
        return lists[0, b, s] + base

    def distances(b, d_ref, wide):
        b = jnp.minimum(b, PB - 1)
        for s in range(0, COLS, 2):
            pair = jnp.concatenate([source[pick(b, s)], source[pick(b, s + 1)]], axis=1)
            d_ref[:, s * TILE : (s + 2) * TILE] = jnp.dot(
                target[b], pair, preferred_element_type=jnp.float32
            )
        wide[...] = jnp.broadcast_to(props[PB + b, 4:5, :], (TILE, TILE)).T

    def weigh(b, d_ref, wide):
        total = []
        hs = [props[pick(b, s), 4:5, :] for s in range(COLS)]
        ms = [props[pick(b, s), 3:4, :] * (8.0 * KERNEL_NORM) for s in range(COLS)]
        for r in range(0, TILE, 16):
            part = None
            mine = wide[r : r + 16, :]
            for s in range(COLS):
                d2 = jnp.maximum(d_ref[r : r + 16, s * TILE : (s + 1) * TILE], 1e-20)
                inverse = pl.reciprocal(mine + hs[s], approx=True)
                t = d2 * lax.rsqrt(d2) * inverse
                fall = jnp.maximum(1.0 - t, 0.0)
                fall = fall * fall
                fall = fall * fall
                value = (fall * (1.0 + 4.0 * t)) * (inverse * inverse * (inverse * ms[s]))
                part = value if part is None else part + value
            total.append(part)
        whole = jnp.concatenate(total, axis=0)
        out[pl.ds(b, 1), :] = jnp.sum(whole.T, axis=0, keepdims=True)

    distances(0, d_even, wide_even)

    def turn(i, _):
        b = 2 * i
        distances(b + 1, d_odd, wide_odd)
        weigh(b, d_even, wide_even)
        distances(b + 2, d_even, wide_even)
        weigh(b + 1, d_odd, wide_odd)
        return 0

    lax.fori_loop(0, PB // 2, turn, 0)


def potential_kernel(
    place, owners, got, back, hot_phi, energy, offs, dense, phis, source, target, mass, sums, d_even, d_odd
):
    me = place[0]
    lane = lanes((8, TILE))
    row = rows((8, TILE))
    labels = got[:, 13, :]
    least = jnp.min(labels)
    agreed = least == jnp.max(labels)
    hot = jnp.maximum(least.astype(jnp.int32), 0)
    mine = agreed & (owners[0, hot] == me)

    at = jnp.int32(0)
    held = jnp.zeros((8, TILE), jnp.float32)
    for s in range(PB):
        q, r = at // TILE, at % TILE
        offs[s] = at
        rolled = pltpu.roll(got[s, 0:8, :], r, 1)
        merged = jnp.where(lane < r, held, rolled)
        dense[q] = merged
        dense[q + 1] = rolled
        at = at + got[s, 5:6, 0:1][0, 0].astype(jnp.int32)
        held = jnp.where(at // TILE == q, merged, rolled)
    total = at
    total = jnp.where(mine, 0, total)
    n_targets = (total + TILE - 1) // TILE
    n_steps = (total + STEP - 1) // STEP

    def prepare(block, c_step, c_lane, c_target, valid):
        block = jnp.where(valid, block, jnp.where(row == 4, 1.0, 0.0))
        coords = jnp.where(row < 3, block - 0.5, 0.0)
        soft = 0.125 * block[4:5, :] * block[4:5, :]
        f, g = factors(coords, soft)
        if c_lane is not None:
            cut = slice(c_lane * TILE, (c_lane + 1) * TILE)
            source[c_step, :, cut] = g.astype(jnp.bfloat16)
            mass[c_step, :, cut] = jnp.broadcast_to(block[3:4, :], (8, TILE))
        if c_target is not None:
            target[c_target] = f.T.astype(jnp.bfloat16)
            sums[c_target] = jnp.zeros((TILE, TILE), jnp.float32)

    def own_step(j, _):
        for i in range(PER_STEP):
            c = j * PER_STEP + i
            prepare(dense[c], j, i, c, lane + c * TILE < total)
        return 0

    lax.fori_loop(0, n_steps, own_step, 0)

    def hot_step(j, _):
        for i in range(PER_STEP):
            prepare(got[j * PER_STEP + i, 8:16, :], STEPS + j, i, None, lane >= 0)
        return 0

    n_hot = jnp.where(agreed, STEPS, 0)
    lax.fori_loop(0, n_hot, hot_step, 0)
    hot_block = got[me, 8:16, :]
    prepare(hot_block, None, None, PB, lane >= 0)
    n_own = n_targets * n_steps
    n_all = n_own + n_hot

    def following(ti, sj):
        end = sj + 1 == jnp.where(ti == PB, STEPS + STEPS, n_steps)
        ti2 = jnp.where(end, ti + 1, ti)
        sj2 = jnp.where(end, 0, sj + 1)
        to_hot = end & (ti2 == n_targets) & (ti < PB)
        return (
            jnp.minimum(jnp.where(to_hot, PB, ti2), PB),
            jnp.minimum(jnp.where(to_hot, STEPS, sj2), 2 * STEPS - 1),
        )

    def distances(ti, sj, d_ref):
        d_ref[...] = jnp.dot(target[ti], source[sj], preferred_element_type=jnp.float32)

    def weigh(t, ti, sj, d_ref):
        slot = jnp.where(t < n_all, ti, PB + 1)
        for r in range(0, TILE, 16):
            value = None
            for i in range(PER_STEP):
                cut = slice(i * TILE, (i + 1) * TILE)
                m = jnp.concatenate([mass[sj, :, cut]] * 2, axis=0)
                term = lax.rsqrt(d_ref[r : r + 16, cut]) * m
                value = term if value is None else value + term
            sums[slot, r : r + 16, :] += value

    start_t = jnp.where(n_own > 0, 0, PB)
    start_s = jnp.where(n_own > 0, 0, STEPS)

    def turn(i, carry):
        ti, sj = carry
        ti2, sj2 = following(ti, sj)
        ti3, sj3 = following(ti2, sj2)
        distances(ti2, sj2, d_odd)
        weigh(2 * i, ti, sj, d_even)
        distances(ti3, sj3, d_even)
        weigh(2 * i + 1, ti2, sj2, d_odd)
        return ti3, sj3

    distances(start_t, start_s, d_even)
    lax.fori_loop(0, (n_all + 1) // 2, turn, (start_t, start_s))

    def finish(c, block):
        summed = jnp.sum(sums[c].T, axis=0, keepdims=True)
        return 2.0 * block[3:4, :] / block[4:5, :] - summed

    def own_finish(c, carry):
        block = dense[c]
        phi = finish(c, block)
        phis[pl.ds(c, 1), :] = phi
        live = lanes((1, TILE)) + c * TILE < total
        return carry + jnp.where(live, block[3:4, :] * phi, 0.0)

    carry = lax.fori_loop(0, n_targets, own_finish, jnp.zeros((1, TILE), jnp.float32))
    energy[...] = jnp.broadcast_to(0.5 * jnp.sum(carry, axis=1, keepdims=True), energy.shape)
    phi = finish(PB, hot_block)
    share = 0.5 * jnp.sum(hot_block[3:4, :] * phi, axis=1, keepdims=True)
    share = jnp.broadcast_to(share, (1, TILE))
    narrow = lanes((1, TILE))
    eight = rows((8, TILE))
    hot_phi[...] = jnp.where(
        eight == 0, phi, jnp.where(agreed, least, -1.0)
    )

    for s in range(PB):
        at = offs[s]
        q, r = at // TILE, at % TILE
        both = jnp.where(narrow >= r, phis[pl.ds(q, 1), :], phis[pl.ds(q + 1, 1), :])
        back[s, 0:1, :] = pltpu.roll(both, (TILE - r) % TILE, 1)
        back[s, 1:2, :] = share


def unpack_kernel(place, counts, owners, back, hot_phi, energy_in, out, energy):
    me = place[0]
    hot = jnp.max(hot_phi[1:2, :]).astype(jnp.int32)
    lane = lanes((1, TILE))
    out[...] = jnp.zeros(out.shape, jnp.float32)
    special = hot_phi[0:1, :]

    def group(k, carry):
        at, held = carry
        count = counts[0, k]
        q, r = at // TILE, at % TILE
        value = jnp.where(k == hot, special, back[owners[0, k], 0:1, :])
        value = jnp.where(lane < count, value, 0.0)
        rolled = pltpu.roll(value, r, 1)
        merged = jnp.where(lane < r, held, rolled)
        out[pl.ds(q, 1), :] = merged
        out[pl.ds(q + 1, 1), :] = jnp.where(lane < r, rolled, 0.0)
        after = at + count
        held = jnp.where(after // TILE == q, merged, rolled)
        return after, held

    lax.fori_loop(
        0, GROUPS, group, (jnp.int32(0), jnp.zeros((1, TILE), jnp.float32)), unroll=8
    )
    shares = jnp.sum(back[:, 1, :], axis=0, keepdims=True)
    is_owner = (hot >= 0) & (owners[0, jnp.maximum(hot, 0)] == me)
    energy[...] = jnp.where(is_owner, shares, energy_in[0:1, :])


def per_device(positions, masses, smoothing, block_lists, block_counts, group_owner):
    f32 = jnp.float32
    place = lax.axis_index("slab").astype(jnp.int32).reshape(1)
    blocks, message = pl.pallas_call(
        pack_kernel,
        out_shape=(
            jax.ShapeDtypeStruct((PB, 8, TILE), f32),
            jax.ShapeDtypeStruct((GROUPS, 16, TILE), f32),
        ),
        in_specs=[SMEM, SMEM, VMEM, VMEM, VMEM],
        out_specs=(VMEM, VMEM),
        compiler_params=params(),
        name="pack",
    )(block_counts, group_owner, positions, masses, smoothing)
    slabs = lax.axis_size(("slab", "grp"))
    up = [(i, (i + 1) % slabs) for i in range(slabs)]
    down = [(t, s) for s, t in up]
    below = lax.ppermute(blocks, ("slab", "grp"), up)
    above = lax.ppermute(blocks, ("slab", "grp"), down)
    got = lax.all_to_all(message, "slab", split_axis=0, concat_axis=0, tiled=True)
    density = pl.pallas_call(
        density_kernel,
        out_shape=jax.ShapeDtypeStruct((PB, TILE), f32),
        in_specs=[SMEM, VMEM, VMEM, VMEM],
        out_specs=VMEM,
        scratch_shapes=[
            pltpu.VMEM((3 * PB, 32, TILE), jnp.bfloat16),
            pltpu.VMEM((PB, TILE, 32), jnp.bfloat16),
            pltpu.VMEM((3 * PB, 8, TILE), f32),
            pltpu.VMEM((TILE, COLS * TILE), f32),
            pltpu.VMEM((TILE, COLS * TILE), f32),
            pltpu.VMEM((TILE, TILE), f32),
            pltpu.VMEM((TILE, TILE), f32),
        ],
        compiler_params=params(),
        cost_estimate=pl.CostEstimate(flops=10**10, bytes_accessed=10**6, transcendentals=0),
        name="density",
    )(block_lists, blocks, below, above)
    back, hot_phi, energy = pl.pallas_call(
        potential_kernel,
        out_shape=(
            jax.ShapeDtypeStruct((GROUPS, 2, TILE), f32),
            jax.ShapeDtypeStruct((8, TILE), f32),
            jax.ShapeDtypeStruct((8, TILE), f32),
        ),
        in_specs=[SMEM, SMEM, VMEM],
        out_specs=(VMEM, VMEM, VMEM),
        scratch_shapes=[
            pltpu.SMEM((PB,), jnp.int32),
            pltpu.VMEM((PB + 2 * PER_STEP, 8, TILE), f32),
            pltpu.VMEM((PB + 8, TILE), f32),
            pltpu.VMEM((2 * STEPS, 32, STEP), jnp.bfloat16),
            pltpu.VMEM((PB + 2, TILE, 32), jnp.bfloat16),
            pltpu.VMEM((2 * STEPS, 8, STEP), f32),
            pltpu.VMEM((PB + 2, TILE, TILE), f32),
            pltpu.VMEM((TILE, STEP), f32),
            pltpu.VMEM((TILE, STEP), f32),
        ],
        compiler_params=params(),
        cost_estimate=pl.CostEstimate(flops=10**10, bytes_accessed=10**6, transcendentals=0),
        name="potential",
    )(place, group_owner, got)
    returned = lax.all_to_all(back, "slab", split_axis=0, concat_axis=0, tiled=True)
    potential, energy = pl.pallas_call(
        unpack_kernel,
        out_shape=(
            jax.ShapeDtypeStruct((PB + 8, TILE), f32),
            jax.ShapeDtypeStruct((1, TILE), f32),
        ),
        in_specs=[SMEM, SMEM, SMEM, VMEM, VMEM, VMEM],
        out_specs=(VMEM, VMEM),
        compiler_params=params(),
        name="unpack",
    )(place, block_counts, group_owner, returned, hot_phi, energy)
    return (
        density.reshape(1, -1),
        potential[:PB].reshape(1, -1),
        energy[:, :1],
    )


def solution(mesh):
    placed = (
        P(("slab", "grp"), None, None),
        P(("slab", "grp"), None),
        P(("slab", "grp"), None),
        P(("slab", "grp"), None, None),
        P(("slab", "grp"), None),
        P("grp", None),
    )
    return jax.shard_map(
        per_device,
        mesh=mesh,
        in_specs=placed,
        out_specs=(P(("slab", "grp"), None), P(("slab", "grp"), None), P("grp", "slab")),
        check_vma=False,
    )
```

```python
import functools
import math

import jax
import jax.numpy as jnp
from jax import lax
from jax.experimental import pallas as pl
from jax.experimental.pallas import tpu as pltpu
from jax.sharding import PartitionSpec as P

TILE = 128
PB = 64
KX = 2
KO = 4
COLS = 2 * KX + KO
GROUPS = 64
UNITS = 16
WIDE = 256
FIRST = 32
KERNEL_NORM = 21.0 / (16.0 * math.pi)
VMEM = pl.BlockSpec(memory_space=pltpu.VMEM)
SMEM = pl.BlockSpec(memory_space=pltpu.SMEM)


def params():
    return pltpu.CompilerParams(vmem_limit_bytes=48 * 1024 * 1024)


def lanes(shape):
    return lax.broadcasted_iota(jnp.int32, shape, len(shape) - 1)


def rows(shape):
    return lax.broadcasted_iota(jnp.int32, shape, len(shape) - 2)


def split(value):
    high = value.astype(jnp.bfloat16).astype(jnp.float32)
    return high, value - high


def split3(value):
    first, rest = split(value)
    second, third = split(rest)
    return first, second, third


def place_factors(block, shift, stage, target, source):
    for kind, out in (("target", target), ("source", source)):
        if out is None:
            continue
        for c in range(0, PB, 8):
            highs, lows, norm = [], [], None
            for k in range(3):
                coord = block[c : c + 8, k, :] - 0.5
                if k == 0 and shift:
                    coord = coord + shift
                high, low = split(coord)
                highs.append(high)
                lows.append(low)
                norm = coord * coord if norm is None else norm + coord * coord
            norms = list(split3(norm))
            ones = [jnp.ones_like(norm)] * 3
            if kind == "target":
                lines = highs + highs + lows + norms + ones
            else:
                highs = [-2.0 * v for v in highs]
                lows = [-2.0 * v for v in lows]
                lines = highs + lows + highs + ones + norms
            for k, line in enumerate(lines + [jnp.zeros_like(norm)]):
                stage[c : c + 8, k, :] = line
            out[c : c + 8] = stage[c : c + 8].astype(jnp.bfloat16)


def pack_kernel(counts, owners, pos, mass, smooth, blocks, message):
    for c in range(PB):
        cut = slice(c * TILE, (c + 1) * TILE)
        blocks[c, 0:3, :] = pos[0, :, cut]
        blocks[c, 3:4, :] = mass[:, cut]
        blocks[c, 4:5, :] = smooth[:, cut]
        blocks[c, 5:8, :] = jnp.zeros((3, TILE), jnp.float32)
    lane = lanes((8, TILE))
    row = rows((8, TILE))

    def window(start):
        q = jnp.minimum(start // TILE, PB - 1)
        r = start % TILE
        both = jnp.where(lane >= r, blocks[q], blocks[jnp.minimum(q + 1, PB - 1)])
        return pltpu.roll(both, (TILE - r) % TILE, 1)

    def group(k, carry):
        start, hot, hot_start = carry
        count = counts[0, k]
        value = window(start)
        value = jnp.where((row == 3) & (lane >= count), 0.0, value)
        value = jnp.where(row == 5, count.astype(jnp.float32), value)
        place = owners[0, k]
        message[place, 0] = value[0:4]
        message[place, 1, 0:2, :] = value[4:6]
        first = (count == TILE) & (hot < 0)
        return (
            start + count,
            jnp.where(first, k, hot),
            jnp.where(first, start, hot_start),
        )

    _, hot, hot_start = lax.fori_loop(
        0, GROUPS, group, (jnp.int32(0), jnp.int32(-1), jnp.int32(0)), unroll=8
    )
    value = jnp.where(row == 5, hot.astype(jnp.float32), window(hot_start))
    for d in range(GROUPS):
        message[d, 1, 2:4, :] = value[4:6]
        message[d, 2] = value[0:4]


def contract(a, b):
    return lax.dot_general(a, b, (((0,), (0,)), ((), ())), preferred_element_type=jnp.float32)


def tall(line):
    return jnp.broadcast_to(line, (TILE, TILE)).T


def column_pass(picks, b_first, b_count, targets, own, sources, others, out, buffers, add, up):
    columns = len(picks)
    last = b_first + b_count - 1

    def distances(b, buffer):
        d_ref, wide_h, wide_m = buffer
        b = jnp.minimum(b, last)
        factor = targets[b]
        for s in range(0, columns, 2):
            pair = jnp.concatenate([sources[picks[s](b)], sources[picks[s + 1](b)]], axis=1)
            d_ref[:, s * TILE : (s + 2) * TILE] = contract(factor, pair)
        wide_h[...] = tall(own[b, 4:5, :])
        if up is not None:
            wide_m[...] = tall(own[b, 3:4, :] * (32.0 * KERNEL_NORM))

    def weigh(b, buffer):
        d_ref, wide_h, wide_m = buffer
        where = [pick(b) for pick in picks]
        hs = [others[c, 4:5, :] for c in where]
        ms = [others[c, 3:4, :] * (1.0 if up is not None else 32.0 * KERNEL_NORM) for c in where]
        total = []
        upward = [None] * columns
        for r in range(0, TILE, 8):
            part = None
            mine = wide_h[r : r + 8, :]
            for s in range(columns):
                d2 = jnp.maximum(d_ref[r : r + 8, s * TILE : (s + 1) * TILE], 1e-20)
                inverse = pl.reciprocal(mine + hs[s], approx=True)
                t = d2 * lax.rsqrt(d2) * inverse
                fall = jnp.maximum(1.0 - t, 0.0)
                fall = fall * fall
                fall = fall * fall
                shape = fall * (0.25 + t)
                if up is None:
                    value = shape * ((inverse * inverse) * (inverse * ms[s]))
                else:
                    value = shape * (inverse * inverse * inverse)
                    send = value * wide_m[r : r + 8, :]
                    upward[s] = send if upward[s] is None else upward[s] + send
                    value = value * ms[s]
                part = value if part is None else part + value
            total.append(part)
        whole = jnp.concatenate(total, axis=0)
        line = jnp.sum(whole.T, axis=0, keepdims=True)
        if up is not None:
            line = line * (32.0 * KERNEL_NORM)
            for s in range(columns):
                up[where[s]] += upward[s]
        if add:
            line = line + out[pl.ds(b, 1), :]
        out[pl.ds(b, 1), :] = line

    even, odd = buffers
    distances(jnp.int32(b_first), even)

    def turn(i, _):
        b = b_first + 2 * i
        distances(b + 1, odd)
        weigh(b, even)
        distances(b + 2, even)
        weigh(b + 1, odd)
        return 0

    lax.fori_loop(0, b_count // 2, turn, 0)


def picks_of(lists, first, count):
    return [lambda b, s=s: lists[0, b, s] for s in range(first, first + count)]


def cross_kernel(lists, own, above, out, up, target, source, over, up_sum, stage, stage_up, *scratch):
    place_factors(own, 0.0, stage, target, None)
    place_factors(above, 1.0, stage_up, None, over)
    place_factors(own, 0.0, stage, None, source)
    up_sum[...] = jnp.zeros(up_sum.shape, jnp.float32)
    buffers = (scratch[0:3], scratch[3:6])
    column_pass(
        picks_of(lists, KX + KO, KX), 0, PB, target, own, over, above, out, buffers, False, up_sum
    )
    column_pass(
        picks_of(lists, KX, KO), 0, FIRST, target, own, source, own, out, buffers, True, None
    )
    for c in range(0, PB, 8):
        total = up_sum[c : c + 8, 0, :]
        for k in range(1, 8):
            total = total + up_sum[c : c + 8, k, :]
        up[c : c + 8, :] = total


def rest_kernel(lists, own, target, source, part, below, after, out, *scratch):
    out[...] = part[...] + below[...]
    buffers = (scratch[0:3], scratch[3:6])
    column_pass(
        picks_of(lists, KX, KO), FIRST, PB - FIRST, target, own, source, own, out, buffers, True, None
    )


def potential_kernel(
    place, owners, got, after, back, hot_phi, energy, offs, dense, phis, source, target, sums, hot_sums, aims, gives
):
    me = place[0]
    lane = lanes((8, TILE))
    row = rows((8, TILE))
    labels = got[:, 1, 3, :]
    least = jnp.min(labels)
    agreed = least == jnp.max(labels)
    hot = jnp.maximum(least.astype(jnp.int32), 0)
    mine = agreed & (owners[0, hot] == me)

    at = jnp.int32(0)
    held = jnp.zeros((8, TILE), jnp.float32)
    for s in range(PB):
        q, r = at // TILE, at % TILE
        offs[s] = at
        block = jnp.concatenate([got[s, 0], got[s, 1]], axis=0)
        rolled = pltpu.roll(block, r, 1)
        merged = jnp.where(lane < r, held, rolled)
        dense[q] = merged
        dense[q + 1] = rolled
        at = at + got[s, 1, 1:2, 0:1][0, 0].astype(jnp.int32)
        held = jnp.where(at // TILE == q, merged, rolled)
    total = at
    total = jnp.where(mine, 0, total)
    n_tiles = (total + WIDE - 1) // WIDE
    n_all = n_tiles * n_tiles
    one = jnp.ones((8, TILE), jnp.float32)

    def pieces(coords, m, h, valid, aims, gives):
        norm = 0.125 * h * h
        for v in coords:
            norm = norm + v * v
        scale = 1.0 / (m * m)
        n0, n1, n2 = split3(norm)
        w0, w1, w2 = split3(scale)
        cost = scale * norm
        if valid is not None:
            cost = jnp.where(valid, cost, 1e30)
        g0, g1, g2 = split3(cost)
        parts = [split(v) for v in coords]
        sent = [split(-2.0 * scale * v) for v in coords]
        if aims is not None:
            lines = [p[0] for p in parts] * 2 + [p[1] for p in parts]
            lines += [n0, n0, n0, n1, n1, n2, one, one, one]
            for k, line in enumerate(lines):
                aims[:, k, :] = line
        if gives is not None:
            lines = [p[0] for p in sent] + [p[1] for p in sent] + [p[0] for p in sent]
            lines += [w0, w1, w2, w0, w1, w0, g0, g1, g2]
            for k, line in enumerate(lines):
                gives[:, k, :] = line

    aims[:, 16:32, :] = jnp.zeros((8, 16, TILE), jnp.float32)
    gives[:, 16:32, :] = jnp.zeros((8, 16, TILE), jnp.float32)

    def own_factors(g, _):
        at = pl.multiple_of(g * 8, 8)
        index = (at + row) * TILE + lane
        valid = index < total
        coords = [jnp.where(valid, dense[pl.ds(at, 8), k, :] - 0.5, 0.0) for k in range(3)]
        m = jnp.where(valid, dense[pl.ds(at, 8), 3, :], 1.0)
        h = jnp.where(valid, dense[pl.ds(at, 8), 4, :], 1.0)
        pieces(coords, m, h, valid, aims, gives)
        for i in range(8):
            tile = g * 4 + i // 2
            cut = slice((i % 2) * TILE, (i % 2 + 1) * TILE)
            target[tile, :, cut] = aims[i].astype(jnp.bfloat16)
            source[tile, cut, :] = gives[i].T.astype(jnp.bfloat16)
            if i % 2 == 0:
                sums[tile] = jnp.zeros((8, WIDE), jnp.float32)
        return 0

    lax.fori_loop(0, (total + 8 * TILE - 1) // (8 * TILE), own_factors, 0)

    def added(d):
        parts = [None] * 4
        for n in range(d.shape[0] // 8):
            term = lax.rsqrt(d[8 * n : 8 * n + 8, :])
            parts[n % 4] = term if parts[n % 4] is None else parts[n % 4] + term
        return (parts[0] + parts[1]) + (parts[2] + parts[3])

    def turn(i, carry):
        ti, sj = carry
        units = []
        for u in range(UNITS):
            units.append((jnp.where(i * UNITS + u < n_all, ti, PB // 2), sj))
            end = sj + 1 >= n_tiles
            ti, sj = jnp.where(end, ti + 1, ti), jnp.where(end, 0, sj + 1)
        for slot, other in units:
            d = jnp.dot(source[other], target[slot], preferred_element_type=jnp.float32)
            sums[slot] += added(d)
        return ti, sj

    lax.fori_loop(0, (n_all + UNITS - 1) // UNITS, turn, (jnp.int32(0), jnp.int32(0)))

    hot_block = jnp.concatenate([got[me, 2], got[me, 1, 2:4, :], got[me, 1, 2:4, :]], axis=0)
    hot_sums[...] = jnp.zeros((8, TILE), jnp.float32)

    @pl.when(agreed)
    def _():
        for g in range(8):
            cut = slice(g * 8, g * 8 + 8)
            coords = [got[cut, 2, k, :] - 0.5 for k in range(3)]
            pieces(coords, got[cut, 2, 3, :], got[cut, 1, 2, :], None, None, gives)
            for i in range(8):
                half = slice((i % 2) * TILE, (i % 2 + 1) * TILE)
                source[g * 4 + i // 2, half, :] = gives[i].T.astype(jnp.bfloat16)
        coords = [got[me, 2, k : k + 1, :] - 0.5 for k in range(3)]
        coords = [jnp.broadcast_to(v, (8, TILE)) for v in coords]
        m = jnp.broadcast_to(hot_block[3:4], (8, TILE))
        h = jnp.broadcast_to(hot_block[4:5], (8, TILE))
        pieces(coords, m, h, None, aims, None)
        aim = aims[0].astype(jnp.bfloat16)
        for j in range(PB // 2):
            hot_sums[...] += added(jnp.dot(source[j], aim, preferred_element_type=jnp.float32))

    def finish(block, summed):
        return 2.0 * block[3:4, :] / block[4:5, :] - jnp.sum(summed, axis=0, keepdims=True)

    def own_finish(t, carry):
        for half in range(2):
            c = 2 * t + half
            block = dense[c]
            phi = finish(block, sums[t, :, half * TILE : (half + 1) * TILE])
            phis[pl.ds(c, 1), :] = phi
            live = lanes((1, TILE)) + c * TILE < total
            carry = carry + jnp.where(live, block[3:4, :] * phi, 0.0)
        return carry

    carry = lax.fori_loop(0, n_tiles, own_finish, jnp.zeros((1, TILE), jnp.float32))
    energy[...] = jnp.broadcast_to(0.5 * jnp.sum(carry, axis=1, keepdims=True), energy.shape)
    phi = finish(hot_block, hot_sums[...])
    share = 0.5 * jnp.sum(hot_block[3:4, :] * phi, axis=1, keepdims=True)
    share = jnp.broadcast_to(share, (1, TILE))
    narrow = lanes((1, TILE))
    eight = rows((8, TILE))
    hot_phi[...] = jnp.where(eight == 0, phi, jnp.where(agreed, least, -1.0))

    for s in range(PB):
        at = offs[s]
        q, r = at // TILE, at % TILE
        both = jnp.where(narrow >= r, phis[pl.ds(q, 1), :], phis[pl.ds(q + 1, 1), :])
        back[s, 0:1, :] = pltpu.roll(both, (TILE - r) % TILE, 1)
        back[s, 1:2, :] = share


def unpack_kernel(place, counts, owners, back, hot_phi, energy_in, result, energy, out):
    me = place[0]
    hot = jnp.max(hot_phi[1:2, :]).astype(jnp.int32)
    lane = lanes((1, TILE))
    out[...] = jnp.zeros(out.shape, jnp.float32)
    special = hot_phi[0:1, :]

    def group(k, carry):
        at, held = carry
        count = counts[0, k]
        q, r = at // TILE, at % TILE
        value = jnp.where(k == hot, special, back[owners[0, k], 0:1, :])
        value = jnp.where(lane < count, value, 0.0)
        rolled = pltpu.roll(value, r, 1)
        merged = jnp.where(lane < r, held, rolled)
        out[pl.ds(q, 1), :] = merged
        out[pl.ds(q + 1, 1), :] = jnp.where(lane < r, rolled, 0.0)
        after = at + count
        held = jnp.where(after // TILE == q, merged, rolled)
        return after, held

    lax.fori_loop(
        0, GROUPS, group, (jnp.int32(0), jnp.zeros((1, TILE), jnp.float32)), unroll=8
    )
    result[...] = out[0:PB, :]
    shares = jnp.sum(back[:, 1, :], axis=0, keepdims=True)
    is_owner = (hot >= 0) & (owners[0, jnp.maximum(hot, 0)] == me)
    energy[...] = jnp.where(is_owner, shares, energy_in[0:1, :])


def per_device(positions, masses, smoothing, block_lists, block_counts, group_owner):
    f32 = jnp.float32
    place = lax.axis_index("slab").astype(jnp.int32).reshape(1)
    blocks, message = pl.pallas_call(
        pack_kernel,
        out_shape=(
            jax.ShapeDtypeStruct((PB, 8, TILE), f32),
            jax.ShapeDtypeStruct((GROUPS, 3, 4, TILE), f32),
        ),
        in_specs=[SMEM, SMEM, VMEM, VMEM, VMEM],
        out_specs=(VMEM, VMEM),
        compiler_params=params(),
        name="pack",
    )(block_counts, group_owner, positions, masses, smoothing)
    slabs = lax.axis_size(("slab", "grp"))
    up = [(i, (i + 1) % slabs) for i in range(slabs)]
    down = [(t, s) for s, t in up]
    above = lax.ppermute(blocks, ("slab", "grp"), down)
    got = lax.all_to_all(message, "slab", split_axis=0, concat_axis=0, tiled=True)
    buffers = [
        pltpu.VMEM((TILE, KO * TILE), f32),
        pltpu.VMEM((TILE, TILE), f32),
        pltpu.VMEM((TILE, TILE), f32),
    ] * 2
    lines = jax.ShapeDtypeStruct((PB, TILE), f32)
    pieces = jax.ShapeDtypeStruct((PB, 16, TILE), jnp.bfloat16)
    cost = pl.CostEstimate(flops=10**10, bytes_accessed=10**6, transcendentals=0)
    part, upward, target, source = pl.pallas_call(
        cross_kernel,
        out_shape=(lines, lines, pieces, pieces),
        in_specs=[SMEM, VMEM, VMEM],
        out_specs=(VMEM, VMEM, VMEM, VMEM),
        scratch_shapes=[
            pltpu.VMEM((PB, 16, TILE), jnp.bfloat16),
            pltpu.VMEM((PB, 8, TILE), f32),
            pltpu.VMEM((PB, 16, TILE), f32),
            pltpu.VMEM((PB, 16, TILE), f32),
            *buffers,
        ],
        compiler_params=params(),
        cost_estimate=cost,
        name="cross",
    )(block_lists, blocks, above)
    from_below = lax.ppermute(upward, ("slab", "grp"), up)
    back, hot_phi, energy = pl.pallas_call(
        potential_kernel,
        out_shape=(
            jax.ShapeDtypeStruct((GROUPS, 2, TILE), f32),
            jax.ShapeDtypeStruct((8, TILE), f32),
            jax.ShapeDtypeStruct((8, TILE), f32),
        ),
        in_specs=[SMEM, SMEM, VMEM, pl.BlockSpec(memory_space=pl.ANY)],
        out_specs=(VMEM, VMEM, VMEM),
        scratch_shapes=[
            pltpu.SMEM((PB,), jnp.int32),
            pltpu.VMEM((PB + 8, 8, TILE), f32),
            pltpu.VMEM((PB + 8, TILE), f32),
            pltpu.VMEM((PB // 2, WIDE, 32), jnp.bfloat16),
            pltpu.VMEM((PB // 2 + 1, 32, WIDE), jnp.bfloat16),
            pltpu.VMEM((PB // 2 + 1, 8, WIDE), f32),
            pltpu.VMEM((8, TILE), f32),
            pltpu.VMEM((8, 32, TILE), f32),
            pltpu.VMEM((8, 32, TILE), f32),
        ],
        compiler_params=params(),
        cost_estimate=cost,
        name="potential",
    )(place, group_owner, got, part)
    density = pl.pallas_call(
        rest_kernel,
        out_shape=lines,
        in_specs=[SMEM, VMEM, VMEM, VMEM, VMEM, VMEM, pl.BlockSpec(memory_space=pl.ANY)],
        out_specs=VMEM,
        scratch_shapes=buffers,
        compiler_params=params(),
        cost_estimate=cost,
        name="rest",
    )(block_lists, blocks, target, source, part, from_below, hot_phi)
    returned = lax.all_to_all(back, "slab", split_axis=0, concat_axis=0, tiled=True)
    potential, energy = pl.pallas_call(
        unpack_kernel,
        out_shape=(
            jax.ShapeDtypeStruct((PB, TILE), f32),
            jax.ShapeDtypeStruct((1, TILE), f32),
        ),
        in_specs=[SMEM, SMEM, SMEM, VMEM, VMEM, VMEM],
        out_specs=(VMEM, VMEM),
        scratch_shapes=[pltpu.VMEM((PB + 8, TILE), f32)],
        compiler_params=params(),
        name="unpack",
    )(place, block_counts, group_owner, returned, hot_phi, energy)
    return (
        density.reshape(1, -1),
        potential.reshape(1, -1),
        energy[:, :1],
    )


def solution(mesh):
    placed = (
        P(("slab", "grp"), None, None),
        P(("slab", "grp"), None),
        P(("slab", "grp"), None),
        P(("slab", "grp"), None, None),
        P(("slab", "grp"), None),
        P("grp", None),
    )
    return jax.shard_map(
        per_device,
        mesh=mesh,
        in_specs=placed,
        out_specs=(P(("slab", "grp"), None), P(("slab", "grp"), None), P("grp", "slab")),
        check_vma=False,
    )
```

```python
import functools
import math

import jax
import jax.numpy as jnp
from jax import lax
from jax.experimental import pallas as pl
from jax.experimental.pallas import tpu as pltpu
from jax.sharding import PartitionSpec as P

TILE = 128
PB = 64
KX = 2
KO = 4
COLS = 2 * KX + KO
GROUPS = 64
UNITS = 16
WIDE = 256
FIRST = 42
CROSS_UNROLL = 16
OWN_UNROLL = 14
KERNEL_NORM = 21.0 / (16.0 * math.pi)
VMEM = pl.BlockSpec(memory_space=pltpu.VMEM)
SMEM = pl.BlockSpec(memory_space=pltpu.SMEM)


def params(size=32):
    return pltpu.CompilerParams(vmem_limit_bytes=size * 1024 * 1024)


def lanes(shape):
    return lax.broadcasted_iota(jnp.int32, shape, len(shape) - 1)


def rows(shape):
    return lax.broadcasted_iota(jnp.int32, shape, len(shape) - 2)


def split(value):
    high = value.astype(jnp.bfloat16).astype(jnp.float32)
    return high, value - high


def split3(value):
    first, rest = split(value)
    second, third = split(rest)
    return first, second, third


def place_factors(block, shift, stage, target, source):
    for kind, out in (("target", target), ("source", source)):
        if out is None:
            continue
        for c in range(0, PB, 8):
            highs, lows, norm = [], [], None
            for k in range(3):
                coord = block[c : c + 8, k, :] - 0.5
                if k == 0 and shift:
                    coord = coord + shift
                high, low = split(coord)
                highs.append(high)
                lows.append(low)
                norm = coord * coord if norm is None else norm + coord * coord
            norms = list(split3(norm))
            ones = [jnp.ones_like(norm)] * 3
            if kind == "target":
                lines = highs + highs + lows + norms + ones
            else:
                highs = [-2.0 * v for v in highs]
                lows = [-2.0 * v for v in lows]
                lines = highs + lows + highs + ones + norms
            for k, line in enumerate(lines + [jnp.zeros_like(norm)]):
                stage[c : c + 8, k, :] = line
            out[c : c + 8] = stage[c : c + 8].astype(jnp.bfloat16)


def pack_kernel(counts, owners, pos, mass, smooth, blocks, message):
    for k, part in enumerate([pos[0], pos[1], pos[2], mass[...], smooth[...]]):
        blocks[:, k, :] = part
    for k in range(5, 8):
        blocks[:, k, :] = jnp.zeros((PB, TILE), jnp.float32)
    lane = lanes((8, TILE))
    row = rows((8, TILE))

    def window(start):
        q = jnp.minimum(start // TILE, PB - 1)
        r = start % TILE
        both = jnp.where(lane >= r, blocks[q], blocks[jnp.minimum(q + 1, PB - 1)])
        return pltpu.roll(both, (TILE - r) % TILE, 1)

    def group(k, carry):
        start, hot, hot_start = carry
        count = counts[0, k]
        value = window(start)
        value = jnp.where((row == 3) & (lane >= count), 0.0, value)
        note = jnp.where(lane == 0, count, k).astype(jnp.float32)
        value = jnp.where(row == 5, note, value)
        place = owners[0, k]
        message[place, 0] = value[0:4]
        message[place, 1, 0:2, :] = value[4:6]
        first = (count == TILE) & (hot < 0)
        return (
            start + count,
            jnp.where(first, k, hot),
            jnp.where(first, start, hot_start),
        )

    _, hot, hot_start = lax.fori_loop(
        0, GROUPS, group, (jnp.int32(0), jnp.int32(-1), jnp.int32(0)), unroll=8
    )
    value = jnp.where(row == 5, hot.astype(jnp.float32), window(hot_start))
    for d in range(GROUPS):
        message[d, 1, 2:4, :] = value[4:6]
        message[d, 2] = value[0:4]


def contract(a, b):
    return lax.dot_general(a, b, (((0,), (0,)), ((), ())), preferred_element_type=jnp.float32)


def tall(line):
    return jnp.broadcast_to(line, (TILE, TILE)).T


def column_pass(picks, b_first, b_count, targets, own, sources, others, out, buffers, add, up):
    columns = len(picks)
    last = b_first + b_count - 1

    def distances(b, buffer):
        d_ref, wide_h, wide_m = buffer
        b = jnp.minimum(b, last)
        factor = targets[b]
        for s in range(0, columns, 2):
            pair = jnp.concatenate([sources[picks[s](b)], sources[picks[s + 1](b)]], axis=1)
            d_ref[:, s * TILE : (s + 2) * TILE] = contract(factor, pair)
        wide_h[...] = tall(own[b, 4:5, :])

    def weigh(b, buffer):
        d_ref, wide_h, wide_m = buffer
        where = [pick(b) for pick in picks]
        hs = [others[c, 4:5, :] for c in where]
        ms = [others[c, 3:4, :] * (1.0 if up is not None else 32.0 * KERNEL_NORM) for c in where]
        total = []
        upward = [None] * columns
        for r in range(0, TILE, 8):
            part = None
            mine = wide_h[r : r + 8, :]
            for s in range(columns):
                d2 = jnp.maximum(d_ref[r : r + 8, s * TILE : (s + 1) * TILE], 1e-20)
                inverse = pl.reciprocal(mine + hs[s], approx=True)
                t = d2 * lax.rsqrt(d2) * inverse
                fall = jnp.maximum(1.0 - t, 0.0)
                fall = fall * fall
                fall = fall * fall
                shape = fall * (0.25 + t)
                if up is None:
                    value = shape * ((inverse * inverse) * (inverse * ms[s]))
                else:
                    value = shape * (inverse * inverse * inverse)
                    send = value * wide_m[r : r + 8, :]
                    upward[s] = send if upward[s] is None else upward[s] + send
                    value = value * ms[s]
                part = value if part is None else part + value
            total.append(part)
        whole = jnp.concatenate(total, axis=0)
        line = jnp.sum(whole.T, axis=0, keepdims=True)
        if up is not None:
            line = line * (32.0 * KERNEL_NORM)
            for s in range(columns):
                up[where[s]] += upward[s]
        if add:
            line = line + out[pl.ds(b, 1), :]
        out[pl.ds(b, 1), :] = line

    even, odd = buffers
    distances(jnp.int32(b_first), even)

    def turn(i, _):
        b = b_first + 2 * i
        distances(b + 1, odd)
        weigh(b, even)
        distances(b + 2, even)
        weigh(b + 1, odd)
        return 0

    lax.fori_loop(0, b_count // 2, turn, 0)


def weight(d2, reach):
    d2 = jnp.maximum(d2, 1e-20)
    inverse = pl.reciprocal(reach, approx=True)
    t = d2 * lax.rsqrt(d2) * inverse
    fall = jnp.maximum(1.0 - t, 0.0)
    fall = fall * fall
    return (fall * fall) * (0.25 + t), inverse


def place_tall(block, stage, lines, wide):
    zero = jnp.zeros((8, TILE), jnp.float32)
    for c in range(0, PB, 8):
        h = split3(block[c : c + 8, 4, :])
        m = split3(block[c : c + 8, 3, :] * (32.0 * KERNEL_NORM))
        for k, line in enumerate([*h, *m] + [zero] * 10):
            stage[c : c + 8, k, :] = line
        lines[c : c + 8] = stage[c : c + 8].astype(jnp.bfloat16)
    row = rows((16, 2 * TILE))
    lane = lanes((16, 2 * TILE))
    choose = jnp.where((row // 3) == (lane // TILE), 1.0, 0.0).astype(jnp.bfloat16)

    def step(i, _):
        for g in range(16):
            wide[16 * i + g] = contract(lines[16 * i + g], choose)
        return 0

    lax.fori_loop(0, PB // 16, step, 0)


def cross_pass(lists, own, above, target, over, wide, out, up_sum):
    def turn(i, _):
        for g in range(CROSS_UNROLL):
            b = i * CROSS_UNROLL + g
            where = [lists[0, s, b] for s in range(KX)]
            pair = jnp.concatenate([over[c] for c in where], axis=1)
            d = contract(target[b], pair)
            hs = [above[c, 4:5, :] for c in where]
            ms = [above[c, 3:4, :] * (32.0 * KERNEL_NORM) for c in where]
            upward = [None] * KX
            total = []
            for r in range(0, TILE, 8):
                part = None
                for s in range(KX):
                    shape, inverse = weight(
                        d[r : r + 8, s * TILE : (s + 1) * TILE], wide[b, r : r + 8, 0:TILE] + hs[s]
                    )
                    value = shape * (inverse * inverse * inverse)
                    send = value * wide[b, r : r + 8, TILE : 2 * TILE]
                    upward[s] = send if upward[s] is None else upward[s] + send
                    value = value * ms[s]
                    part = value if part is None else part + value
                total.append(part)
            whole = jnp.concatenate(total, axis=0)
            out[pl.ds(b, 1), :] = jnp.sum(whole.T, axis=0, keepdims=True)
            for s in range(KX):
                up_sum[where[s]] += upward[s]
        return 0

    lax.fori_loop(0, PB // CROSS_UNROLL, turn, 0)


def own_pass(lists, own, target, source, wide, sums):
    def turn(i, _):
        for g in range(OWN_UNROLL):
            b = i * OWN_UNROLL + g
            where = [lists[0, KX + s, b] for s in range(KO)]
            d = contract(jnp.concatenate([source[c] for c in where], axis=1), target[b])
            mine = own[b, 4:5, :]
            total = [None] * 4
            for s in range(KO):
                for r in range(0, TILE, 8):
                    shape, inverse = weight(
                        d[s * TILE + r : s * TILE + r + 8, :], wide[where[s], r : r + 8, 0:TILE] + mine
                    )
                    scale = (inverse * inverse) * (inverse * wide[where[s], r : r + 8, TILE : 2 * TILE])
                    total[s] = shape * scale if total[s] is None else total[s] + shape * scale
            sums[b] = (total[0] + total[1]) + (total[2] + total[3])
        return 0

    lax.fori_loop(0, FIRST // OWN_UNROLL, turn, 0)


def folded(block, c):
    total = block[c : c + 8, 0, :]
    for k in range(1, 8):
        total = total + block[c : c + 8, k, :]
    return total


def picks_of(lists, first, count):
    return [lambda b, s=s: lists[0, s, b] for s in range(first, first + count)]


def cross_kernel(
    listed, own, above, out, up, target, source, over, up_sum, stage, stage_up, lines, wide, sums, lists, ready
):
    fetch = pltpu.make_async_copy(listed, lists, ready)
    fetch.start()
    place_tall(own, stage, lines, wide)
    place_factors(own, 0.0, stage_up, target, None)
    place_factors(above, -1.0, stage, None, over)
    place_factors(own, 0.0, stage_up, None, source)
    up_sum[...] = jnp.zeros(up_sum.shape, jnp.float32)
    sums[...] = jnp.zeros(sums.shape, jnp.float32)
    fetch.wait()
    cross_pass(lists, own, above, target, over, wide, out, up_sum)
    own_pass(lists, own, target, source, wide, sums)
    for c in range(0, PB, 8):
        up[c : c + 8, :] = folded(up_sum, c)
        out[c : c + 8, :] += folded(sums, c)


def rest_kernel(lists, own, target, source, part, below, after, out, *scratch):
    out[...] = part[...] + below[...]
    buffers = (scratch[0:3], scratch[3:6])
    column_pass(
        picks_of(lists, KX, KO), FIRST, PB - FIRST, target, own, source, own, out, buffers, True, None
    )


def potential_kernel(
    place, got, after, back, hot_phi, energy, offs, dense, phis, source, target, sums, hot_sums, aims, gives
):
    me = place[0]
    lane = lanes((8, TILE))
    row = rows((8, TILE))
    labels = got[:, 1, 3, :]
    least = jnp.min(labels)
    agreed = least == jnp.max(labels)
    mine = agreed & (least == jnp.max(got[0, 1, 1:2, 1:TILE]))

    at = jnp.int32(0)
    held = jnp.zeros((8, TILE), jnp.float32)
    for s in range(PB):
        q, r = at // TILE, at % TILE
        offs[s] = at
        block = jnp.concatenate([got[s, 0], got[s, 1]], axis=0)
        rolled = pltpu.roll(block, r, 1)
        merged = jnp.where(lane < r, held, rolled)
        dense[q] = merged
        dense[q + 1] = rolled
        at = at + got[s, 1, 1:2, 0:1][0, 0].astype(jnp.int32)
        held = jnp.where(at // TILE == q, merged, rolled)
    total = at
    total = jnp.where(mine, 0, total)
    n_tiles = (total + WIDE - 1) // WIDE
    n_all = n_tiles * n_tiles
    one = jnp.ones((8, TILE), jnp.float32)

    def pieces(coords, m, h, valid, aims, gives):
        norm = 0.125 * h * h
        for v in coords:
            norm = norm + v * v
        scale = 1.0 / (m * m)
        n0, n1, n2 = split3(norm)
        w0, w1, w2 = split3(scale)
        cost = scale * norm
        if valid is not None:
            cost = jnp.where(valid, cost, 1e30)
        g0, g1, g2 = split3(cost)
        parts = [split(v) for v in coords]
        sent = [split(-2.0 * scale * v) for v in coords]
        if aims is not None:
            lines = [p[0] for p in parts] * 2 + [p[1] for p in parts]
            lines += [n0, n0, n0, n1, n1, n2, one, one, one]
            for k, line in enumerate(lines):
                aims[:, k, :] = line
        if gives is not None:
            lines = [p[0] for p in sent] + [p[1] for p in sent] + [p[0] for p in sent]
            lines += [w0, w1, w2, w0, w1, w0, g0, g1, g2]
            for k, line in enumerate(lines):
                gives[:, k, :] = line

    aims[:, 16:32, :] = jnp.zeros((8, 16, TILE), jnp.float32)
    gives[:, 16:32, :] = jnp.zeros((8, 16, TILE), jnp.float32)

    def own_factors(g, _):
        at = pl.multiple_of(g * 8, 8)
        index = (at + row) * TILE + lane
        valid = index < total
        coords = [jnp.where(valid, dense[pl.ds(at, 8), k, :] - 0.5, 0.0) for k in range(3)]
        m = jnp.where(valid, dense[pl.ds(at, 8), 3, :], 1.0)
        h = jnp.where(valid, dense[pl.ds(at, 8), 4, :], 1.0)
        pieces(coords, m, h, valid, aims, gives)
        for i in range(8):
            tile = g * 4 + i // 2
            cut = slice((i % 2) * TILE, (i % 2 + 1) * TILE)
            target[tile, :, cut] = aims[i].astype(jnp.bfloat16)
            source[tile, cut, :] = gives[i].T.astype(jnp.bfloat16)
            if i % 2 == 0:
                sums[tile] = jnp.zeros((8, WIDE), jnp.float32)
        return 0

    lax.fori_loop(0, (total + 8 * TILE - 1) // (8 * TILE), own_factors, 0)

    def added(d):
        parts = [None] * 4
        for n in range(d.shape[0] // 8):
            term = lax.rsqrt(d[8 * n : 8 * n + 8, :])
            parts[n % 4] = term if parts[n % 4] is None else parts[n % 4] + term
        return (parts[0] + parts[1]) + (parts[2] + parts[3])

    def turn(i, carry):
        ti, sj = carry
        units = []
        for u in range(UNITS):
            units.append((jnp.where(i * UNITS + u < n_all, ti, PB // 2), sj))
            end = sj + 1 >= n_tiles
            ti, sj = jnp.where(end, ti + 1, ti), jnp.where(end, 0, sj + 1)
        for slot, other in units:
            d = jnp.dot(source[other], target[slot], preferred_element_type=jnp.float32)
            sums[slot] += added(d)
        return ti, sj

    lax.fori_loop(0, (n_all + UNITS - 1) // UNITS, turn, (jnp.int32(0), jnp.int32(0)))

    hot_block = jnp.concatenate([got[me, 2], got[me, 1, 2:4, :], got[me, 1, 2:4, :]], axis=0)
    hot_sums[...] = jnp.zeros((TILE, TILE), jnp.float32)

    @pl.when(agreed)
    def _():
        for g in range(8):
            cut = slice(g * 8, g * 8 + 8)
            coords = [got[cut, 2, k, :] - 0.5 for k in range(3)]
            pieces(coords, got[cut, 2, 3, :], got[cut, 1, 2, :], None, None, gives)
            for i in range(8):
                half = slice((i % 2) * TILE, (i % 2 + 1) * TILE)
                target[g * 4 + i // 2, :, half] = gives[i].astype(jnp.bfloat16)
        coords = [got[me, 2, k : k + 1, :] - 0.5 for k in range(3)]
        coords = [jnp.broadcast_to(v, (8, TILE)) for v in coords]
        m = jnp.broadcast_to(hot_block[3:4], (8, TILE))
        h = jnp.broadcast_to(hot_block[4:5], (8, TILE))
        pieces(coords, m, h, None, aims, None)
        aim = aims[0].T.astype(jnp.bfloat16)
        for j in range(0, PB // 2, 4):
            total = None
            for u in range(4):
                d = lax.rsqrt(jnp.dot(aim, target[j + u], preferred_element_type=jnp.float32))
                both = d[:, 0:TILE] + d[:, TILE:WIDE]
                total = both if total is None else total + both
            hot_sums[...] += total

    def finish(block, summed):
        return 2.0 * block[3:4, :] / block[4:5, :] - jnp.sum(summed, axis=0, keepdims=True)

    def own_finish(t, carry):
        for half in range(2):
            c = 2 * t + half
            block = dense[c]
            phi = finish(block, sums[t, :, half * TILE : (half + 1) * TILE])
            phis[pl.ds(c, 1), :] = phi
            live = lanes((1, TILE)) + c * TILE < total
            carry = carry + jnp.where(live, block[3:4, :] * phi, 0.0)
        return carry

    carry = lax.fori_loop(0, n_tiles, own_finish, jnp.zeros((1, TILE), jnp.float32))
    energy[...] = jnp.broadcast_to(0.5 * jnp.sum(carry, axis=1, keepdims=True), energy.shape)
    phi = finish(hot_block, hot_sums[...].T)
    share = 0.5 * jnp.sum(hot_block[3:4, :] * phi, axis=1, keepdims=True)
    share = jnp.broadcast_to(share, (1, TILE))
    narrow = lanes((1, TILE))
    eight = rows((8, TILE))
    hot_phi[...] = jnp.where(eight == 0, phi, jnp.where(agreed, least, -1.0))

    for s in range(PB):
        at = offs[s]
        q, r = at // TILE, at % TILE
        both = jnp.where(narrow >= r, phis[pl.ds(q, 1), :], phis[pl.ds(q + 1, 1), :])
        back[s, 0:1, :] = pltpu.roll(both, (TILE - r) % TILE, 1)
        back[s, 1:2, :] = share


def unpack_kernel(place, counts, owners, back, hot_phi, energy_in, result, energy, out):
    me = place[0]
    hot = jnp.max(hot_phi[1:2, :]).astype(jnp.int32)
    lane = lanes((1, TILE))
    out[...] = jnp.zeros(out.shape, jnp.float32)
    special = hot_phi[0:1, :]

    def group(k, carry):
        at, held = carry
        count = counts[0, k]
        q, r = at // TILE, at % TILE
        value = jnp.where(k == hot, special, back[owners[0, k], 0:1, :])
        value = jnp.where(lane < count, value, 0.0)
        rolled = pltpu.roll(value, r, 1)
        merged = jnp.where(lane < r, held, rolled)
        out[pl.ds(q, 1), :] = merged
        out[pl.ds(q + 1, 1), :] = jnp.where(lane < r, rolled, 0.0)
        after = at + count
        held = jnp.where(after // TILE == q, merged, rolled)
        return after, held

    lax.fori_loop(
        0, GROUPS, group, (jnp.int32(0), jnp.zeros((1, TILE), jnp.float32)), unroll=8
    )
    result[...] = out[0:PB, :]
    shares = jnp.sum(back[:, 1, :], axis=0, keepdims=True)
    is_owner = (hot >= 0) & (owners[0, jnp.maximum(hot, 0)] == me)
    energy[...] = jnp.where(is_owner, shares, energy_in[0:1, :])


def per_device(positions, masses, smoothing, block_lists, block_counts, group_owner):
    f32 = jnp.float32
    place = lax.axis_index("slab").astype(jnp.int32).reshape(1)
    lists = block_lists.transpose(0, 2, 1)
    blocks, message = pl.pallas_call(
        pack_kernel,
        out_shape=(
            jax.ShapeDtypeStruct((PB, 8, TILE), f32),
            jax.ShapeDtypeStruct((GROUPS, 3, 4, TILE), f32),
        ),
        in_specs=[SMEM, SMEM, VMEM, VMEM, VMEM],
        out_specs=(VMEM, VMEM),
        compiler_params=params(60),
        name="pack",
    )(
        block_counts,
        group_owner,
        positions.transpose(1, 0, 2).reshape(3, PB, TILE),
        masses.reshape(PB, TILE),
        smoothing.reshape(PB, TILE),
    )
    slabs = lax.axis_size(("slab", "grp"))
    up = [(i, (i + 1) % slabs) for i in range(slabs)]
    down = [(t, s) for s, t in up]
    above = lax.ppermute(blocks, ("slab", "grp"), up)
    got = lax.all_to_all(message, "slab", split_axis=0, concat_axis=0, tiled=True)
    buffers = [
        pltpu.VMEM((TILE, KO * TILE), f32),
        pltpu.VMEM((TILE, TILE), f32),
        pltpu.VMEM((TILE, TILE), f32),
    ] * 2
    lines = jax.ShapeDtypeStruct((PB, TILE), f32)
    pieces = jax.ShapeDtypeStruct((PB, 16, TILE), jnp.bfloat16)
    cost = pl.CostEstimate(flops=10**10, bytes_accessed=10**6, transcendentals=0)
    part, upward, target, source = pl.pallas_call(
        cross_kernel,
        out_shape=(lines, lines, pieces, pieces),
        in_specs=[pl.BlockSpec(memory_space=pl.ANY), VMEM, VMEM],
        out_specs=(VMEM, VMEM, VMEM, VMEM),
        scratch_shapes=[
            pltpu.VMEM((PB, 16, TILE), jnp.bfloat16),
            pltpu.VMEM((PB, 8, TILE), f32),
            pltpu.VMEM((PB, 16, TILE), f32),
            pltpu.VMEM((PB, 16, TILE), f32),
            pltpu.VMEM((PB, 16, TILE), jnp.bfloat16),
            pltpu.VMEM((PB, TILE, 2 * TILE), f32),
            pltpu.VMEM((PB, 8, TILE), f32),
            pltpu.SMEM((1, COLS, PB), jnp.int32),
            pltpu.SemaphoreType.DMA,
        ],
        compiler_params=params(),
        cost_estimate=cost,
        name="cross",
    )(lists, blocks, above)
    from_below = lax.ppermute(upward, ("slab", "grp"), down)
    back, hot_phi, energy = pl.pallas_call(
        potential_kernel,
        out_shape=(
            jax.ShapeDtypeStruct((GROUPS, 2, TILE), f32),
            jax.ShapeDtypeStruct((8, TILE), f32),
            jax.ShapeDtypeStruct((8, TILE), f32),
        ),
        in_specs=[SMEM, VMEM, pl.BlockSpec(memory_space=pl.ANY)],
        out_specs=(VMEM, VMEM, VMEM),
        scratch_shapes=[
            pltpu.SMEM((PB,), jnp.int32),
            pltpu.VMEM((PB + 8, 8, TILE), f32),
            pltpu.VMEM((PB + 8, TILE), f32),
            pltpu.VMEM((PB // 2, WIDE, 32), jnp.bfloat16),
            pltpu.VMEM((PB // 2 + 1, 32, WIDE), jnp.bfloat16),
            pltpu.VMEM((PB // 2 + 1, 8, WIDE), f32),
            pltpu.VMEM((TILE, TILE), f32),
            pltpu.VMEM((8, 32, TILE), f32),
            pltpu.VMEM((8, 32, TILE), f32),
        ],
        compiler_params=params(),
        cost_estimate=cost,
        name="potential",
    )(place, got, part)
    density = pl.pallas_call(
        rest_kernel,
        out_shape=lines,
        in_specs=[SMEM, VMEM, VMEM, VMEM, VMEM, VMEM, pl.BlockSpec(memory_space=pl.ANY)],
        out_specs=VMEM,
        scratch_shapes=buffers,
        compiler_params=params(),
        cost_estimate=cost,
        name="rest",
    )(lists, blocks, target, source, part, from_below, hot_phi)
    returned = lax.all_to_all(back, "slab", split_axis=0, concat_axis=0, tiled=True)
    potential, energy = pl.pallas_call(
        unpack_kernel,
        out_shape=(
            jax.ShapeDtypeStruct((PB, TILE), f32),
            jax.ShapeDtypeStruct((1, TILE), f32),
        ),
        in_specs=[SMEM, SMEM, SMEM, VMEM, VMEM, VMEM],
        out_specs=(VMEM, VMEM),
        scratch_shapes=[pltpu.VMEM((PB + 8, TILE), f32)],
        compiler_params=params(),
        name="unpack",
    )(place, block_counts, group_owner, returned, hot_phi, energy)
    return (
        density.reshape(1, -1),
        potential.reshape(1, -1),
        energy[:, :1],
    )


def solution(mesh):
    placed = (
        P(("slab", "grp"), None, None),
        P(("slab", "grp"), None),
        P(("slab", "grp"), None),
        P(("slab", "grp"), None, None),
        P(("slab", "grp"), None),
        P("grp", None),
    )
    return jax.shard_map(
        per_device,
        mesh=mesh,
        in_specs=placed,
        out_specs=(P(("slab", "grp"), None), P(("slab", "grp"), None), P("grp", "slab")),
        check_vma=False,
    )
```

```python
import functools
import math

import jax
import jax.numpy as jnp
from jax import lax
from jax.experimental import pallas as pl
from jax.experimental.pallas import tpu as pltpu
from jax.sharding import PartitionSpec as P

TILE = 128
PB = 64
KX = 2
KO = 4
COLS = 2 * KX + KO
GROUPS = 64
UNITS = 16
WIDE = 256
FIRST = 32
CROSS_UNROLL = 32
OWN_UNROLL = 16
REST_UNROLL = 16
KERNEL_NORM = 21.0 / (16.0 * math.pi)
VMEM = pl.BlockSpec(memory_space=pltpu.VMEM)
SMEM = pl.BlockSpec(memory_space=pltpu.SMEM)


def params(size=32):
    return pltpu.CompilerParams(vmem_limit_bytes=size * 1024 * 1024)


def lanes(shape):
    return lax.broadcasted_iota(jnp.int32, shape, len(shape) - 1)


def rows(shape):
    return lax.broadcasted_iota(jnp.int32, shape, len(shape) - 2)


def split(value):
    high = value.astype(jnp.bfloat16).astype(jnp.float32)
    return high, value - high


def split3(value):
    first, rest = split(value)
    second, third = split(rest)
    return first, second, third


def place_factors(block, shift, stage, target, source):
    for kind, out in (("target", target), ("source", source)):
        if out is None:
            continue
        for c in range(0, PB, 8):
            highs, lows, norm = [], [], None
            for k in range(3):
                coord = block[c : c + 8, k, :] - 0.5
                if k == 0 and shift:
                    coord = coord + shift
                high, low = split(coord)
                highs.append(high)
                lows.append(low)
                norm = coord * coord if norm is None else norm + coord * coord
            norms = list(split3(norm))
            ones = [jnp.ones_like(norm)] * 3
            if kind == "target":
                lines = highs + highs + lows + norms + ones
            else:
                highs = [-2.0 * v for v in highs]
                lows = [-2.0 * v for v in lows]
                lines = highs + lows + highs + ones + norms
            for k, line in enumerate(lines + [jnp.zeros_like(norm)]):
                stage[c : c + 8, k, :] = line
            out[c : c + 8] = stage[c : c + 8].astype(jnp.bfloat16)


def pack_kernel(counts, owners, pos, mass, smooth, blocks, message):
    for k, part in enumerate([pos[0], pos[1], pos[2], mass[...], smooth[...]]):
        blocks[:, k, :] = part
    for k in range(5, 8):
        blocks[:, k, :] = jnp.zeros((PB, TILE), jnp.float32)
    lane = lanes((8, TILE))
    row = rows((8, TILE))

    def window(start):
        q = jnp.minimum(start // TILE, PB - 1)
        r = start % TILE
        both = jnp.where(lane >= r, blocks[q], blocks[jnp.minimum(q + 1, PB - 1)])
        return pltpu.roll(both, (TILE - r) % TILE, 1)

    def group(k, carry):
        start, hot, hot_start = carry
        count = counts[0, k]
        value = window(start)
        value = jnp.where((row == 3) & (lane >= count), 0.0, value)
        note = jnp.where(lane == 0, count, k).astype(jnp.float32)
        value = jnp.where(row == 5, note, value)
        place = owners[0, k]
        message[place, 0] = value[0:4]
        message[place, 1, 0:2, :] = value[4:6]
        first = (count == TILE) & (hot < 0)
        return (
            start + count,
            jnp.where(first, k, hot),
            jnp.where(first, start, hot_start),
        )

    _, hot, hot_start = lax.fori_loop(
        0, GROUPS, group, (jnp.int32(0), jnp.int32(-1), jnp.int32(0)), unroll=8
    )
    value = jnp.where(row == 5, hot.astype(jnp.float32), window(hot_start))
    for d in range(GROUPS):
        message[d, 1, 2:4, :] = value[4:6]
        message[d, 2] = value[0:4]


def contract(a, b):
    return lax.dot_general(a, b, (((0,), (0,)), ((), ())), preferred_element_type=jnp.float32)


def weight(d2, reach):
    d2 = jnp.maximum(d2, 1e-20)
    inverse = pl.reciprocal(reach, approx=True)
    t = d2 * lax.rsqrt(d2) * inverse
    fall = jnp.maximum(1.0 - t, 0.0)
    fall = fall * fall
    return (fall * fall) * (0.25 + t), inverse


def place_lines(block, stage, lines):
    zero = jnp.zeros((8, TILE), jnp.float32)
    for c in range(0, PB, 8):
        h = split3(block[c : c + 8, 4, :])
        m = split3(block[c : c + 8, 3, :] * (32.0 * KERNEL_NORM))
        for k, line in enumerate([*h, *m] + [zero] * 10):
            stage[c : c + 8, k, :] = line
        lines[c : c + 8] = stage[c : c + 8].astype(jnp.bfloat16)


def place_scaled(block, stage, sources, targets):
    zero = jnp.zeros((8, TILE), jnp.float32)
    one = jnp.ones((8, TILE), jnp.float32)
    for c in range(0, PB, 8):
        cut = slice(c, c + 8)
        coords = [block[cut, k, :] - 0.5 for k in range(3)]
        h = block[cut, 4, :]
        root = jnp.exp(jnp.log(block[cut, 3, :] * (32.0 * KERNEL_NORM)) * (-1.0 / 3.0))
        scale = root * root
        norm = coords[0] * coords[0] + coords[1] * coords[1] + coords[2] * coords[2]
        n0, n1, n2 = split3(norm)
        s0, s1, s2 = split3(scale)
        c0, c1, c2 = split3(root)
        h0, h1, h2 = split3(h)
        parts = [split(v) for v in coords]
        sent = [split(-2.0 * scale * v) for v in coords]
        high, low = [p[0] for p in parts], [p[1] for p in parts]
        give = [p[0] for p in sent] + [p[1] for p in sent] + [p[0] for p in sent]
        give += [s0, s1, s2, s0, s1, s0, *split3(scale * norm)]
        give += [c0, c1, c2, c0, c1, c0, *split3(root * h)]
        aim = high + high + low + [n0, n0, n0, n1, n1, n2, one, one, one] + [zero] * 14
        reach = [zero] * 18 + [h0, h0, h0, h1, h1, h2, one, one, one] + [zero] * 5
        give += [zero] * 5
        for lines, out in ((give, sources.at[cut]), (aim, targets.at[cut, :, 0:TILE]), (reach, targets.at[cut, :, TILE:])):
            for k, line in enumerate(lines):
                stage[cut, k, :] = line
            out[...] = stage[cut].astype(jnp.bfloat16)


def cross_pass(lists, above, target, over, lines, out, up_sum):
    row = rows((16, 2 * TILE))
    lane = lanes((16, 2 * TILE))
    choose = jnp.where((row // 3) == (lane // TILE), 1.0, 0.0).astype(jnp.bfloat16)

    def turn(i, _):
        for g in range(CROSS_UNROLL):
            b = i * CROSS_UNROLL + g
            where = [lists[0, s, b] for s in range(KX)]
            pair = jnp.concatenate([over[c] for c in where], axis=1)
            d = contract(target[b], pair)
            wide = contract(lines[b], choose)
            hs = [above[c, 4:5, :] for c in where]
            ms = [above[c, 3:4, :] * (32.0 * KERNEL_NORM) for c in where]
            upward = [None] * KX
            total = []
            for r in range(0, TILE, 8):
                part = None
                for s in range(KX):
                    shape, inverse = weight(
                        d[r : r + 8, s * TILE : (s + 1) * TILE], wide[r : r + 8, 0:TILE] + hs[s]
                    )
                    value = shape * (inverse * inverse * inverse)
                    send = value * wide[r : r + 8, TILE : 2 * TILE]
                    upward[s] = send if upward[s] is None else upward[s] + send
                    value = value * ms[s]
                    part = value if part is None else part + value
                total.append(part)
            whole = jnp.concatenate(total, axis=0)
            out[pl.ds(b, 1), :] = jnp.sum(whole.T, axis=0, keepdims=True)
            for s in range(KX):
                up_sum[where[s]] += upward[s]
        return 0

    lax.fori_loop(0, PB // CROSS_UNROLL, turn, 0)


def own_pass(lists, first, count, unroll, targets, sources, sums):
    def turn(i, _):
        for g in range(unroll):
            b = first + i * unroll + g
            where = [lists[0, KX + s, b] for s in range(KO)]
            d = contract(jnp.concatenate([sources[c] for c in where], axis=1), targets[b])
            total = [None] * 4
            for n in range(KO * TILE // 8):
                cut = slice(8 * n, 8 * n + 8)
                shape, inverse = weight(d[cut, 0:TILE], d[cut, TILE : 2 * TILE])
                value = shape * (inverse * inverse * inverse)
                total[n % 4] = value if total[n % 4] is None else total[n % 4] + value
            sums[b] = (total[0] + total[1]) + (total[2] + total[3])
        return 0

    lax.fori_loop(0, count // unroll, turn, 0)


def folded(block, c):
    total = block[c : c + 8, 0, :]
    for k in range(1, 8):
        total = total + block[c : c + 8, k, :]
    return total


def cross_kernel(
    listed, own, above, out, up, sources, targets, target, over, up_sum, stage, stage_up, wider, lines, sums, lists, ready
):
    fetch = pltpu.make_async_copy(listed, lists, ready)
    fetch.start()
    place_lines(own, stage, lines)
    place_factors(own, 0.0, stage_up, target, None)
    place_factors(above, -1.0, stage, None, over)
    place_scaled(own, wider, sources, targets)
    up_sum[...] = jnp.zeros(up_sum.shape, jnp.float32)
    sums[...] = jnp.zeros(sums.shape, jnp.float32)
    fetch.wait()
    cross_pass(lists, above, target, over, lines, out, up_sum)
    own_pass(lists, 0, FIRST, OWN_UNROLL, targets, sources, sums)
    for c in range(0, PB, 8):
        up[c : c + 8, :] = folded(up_sum, c)
        out[c : c + 8, :] += folded(sums, c)


def rest_kernel(lists, sources, targets, part, below, after, out, sums):
    sums[...] = jnp.zeros(sums.shape, jnp.float32)
    own_pass(lists, FIRST, PB - FIRST, REST_UNROLL, targets, sources, sums)
    for c in range(0, PB, 8):
        cut = slice(c, c + 8)
        out[cut, :] = part[cut, :] + below[cut, :] + folded(sums, c)


def potential_kernel(
    place, got, after, back, hot_phi, energy, offs, dense, phis, source, target, sums, hot_sums, aims, gives
):
    me = place[0]
    lane = lanes((8, TILE))
    row = rows((8, TILE))
    labels = got[:, 1, 3, :]
    least = jnp.min(labels)
    agreed = least == jnp.max(labels)
    mine = agreed & (least == jnp.max(got[0, 1, 1:2, 1:TILE]))

    at = jnp.int32(0)
    held = jnp.zeros((8, TILE), jnp.float32)
    for s in range(PB):
        q, r = at // TILE, at % TILE
        offs[s] = at
        block = jnp.concatenate([got[s, 0], got[s, 1]], axis=0)
        rolled = pltpu.roll(block, r, 1)
        merged = jnp.where(lane < r, held, rolled)
        dense[q] = merged
        dense[q + 1] = rolled
        at = at + got[s, 1, 1:2, 0:1][0, 0].astype(jnp.int32)
        held = jnp.where(at // TILE == q, merged, rolled)
    total = at
    total = jnp.where(mine, 0, total)
    n_tiles = (total + WIDE - 1) // WIDE
    n_all = n_tiles * n_tiles
    one = jnp.ones((8, TILE), jnp.float32)

    def pieces(coords, m, h, valid, aims, gives):
        norm = 0.125 * h * h
        for v in coords:
            norm = norm + v * v
        scale = 1.0 / (m * m)
        n0, n1, n2 = split3(norm)
        w0, w1, w2 = split3(scale)
        cost = scale * norm
        if valid is not None:
            cost = jnp.where(valid, cost, 1e30)
        g0, g1, g2 = split3(cost)
        parts = [split(v) for v in coords]
        sent = [split(-2.0 * scale * v) for v in coords]
        if aims is not None:
            lines = [p[0] for p in parts] * 2 + [p[1] for p in parts]
            lines += [n0, n0, n0, n1, n1, n2, one, one, one]
            for k, line in enumerate(lines):
                aims[:, k, :] = line
        if gives is not None:
            lines = [p[0] for p in sent] + [p[1] for p in sent] + [p[0] for p in sent]
            lines += [w0, w1, w2, w0, w1, w0, g0, g1, g2]
            for k, line in enumerate(lines):
                gives[:, k, :] = line

    aims[:, 16:32, :] = jnp.zeros((8, 16, TILE), jnp.float32)
    gives[:, 16:32, :] = jnp.zeros((8, 16, TILE), jnp.float32)

    def own_factors(g, _):
        at = pl.multiple_of(g * 8, 8)
        index = (at + row) * TILE + lane
        valid = index < total
        coords = [jnp.where(valid, dense[pl.ds(at, 8), k, :] - 0.5, 0.0) for k in range(3)]
        m = jnp.where(valid, dense[pl.ds(at, 8), 3, :], 1.0)
        h = jnp.where(valid, dense[pl.ds(at, 8), 4, :], 1.0)
        pieces(coords, m, h, valid, aims, gives)
        for i in range(8):
            tile = g * 4 + i // 2
            cut = slice((i % 2) * TILE, (i % 2 + 1) * TILE)
            target[tile, :, cut] = aims[i].astype(jnp.bfloat16)
            source[tile, cut, :] = gives[i].T.astype(jnp.bfloat16)
            if i % 2 == 0:
                sums[tile] = jnp.zeros((8, WIDE), jnp.float32)
        return 0

    lax.fori_loop(0, (total + 8 * TILE - 1) // (8 * TILE), own_factors, 0)

    def added(d):
        parts = [None] * 4
        for n in range(d.shape[0] // 8):
            term = lax.rsqrt(d[8 * n : 8 * n + 8, :])
            parts[n % 4] = term if parts[n % 4] is None else parts[n % 4] + term
        return (parts[0] + parts[1]) + (parts[2] + parts[3])

    def turn(i, carry):
        ti, sj = carry
        units = []
        for u in range(UNITS):
            units.append((jnp.where(i * UNITS + u < n_all, ti, PB // 2), sj))
            end = sj + 1 >= n_tiles
            ti, sj = jnp.where(end, ti + 1, ti), jnp.where(end, 0, sj + 1)
        for slot, other in units:
            d = jnp.dot(source[other], target[slot], preferred_element_type=jnp.float32)
            sums[slot] += added(d)
        return ti, sj

    lax.fori_loop(0, (n_all + UNITS - 1) // UNITS, turn, (jnp.int32(0), jnp.int32(0)))

    hot_block = jnp.concatenate([got[me, 2], got[me, 1, 2:4, :], got[me, 1, 2:4, :]], axis=0)
    hot_sums[...] = jnp.zeros((TILE, TILE), jnp.float32)

    @pl.when(agreed)
    def _():
        for g in range(8):
            cut = slice(g * 8, g * 8 + 8)
            coords = [got[cut, 2, k, :] - 0.5 for k in range(3)]
            pieces(coords, got[cut, 2, 3, :], got[cut, 1, 2, :], None, None, gives)
            for i in range(8):
                half = slice((i % 2) * TILE, (i % 2 + 1) * TILE)
                target[g * 4 + i // 2, :, half] = gives[i].astype(jnp.bfloat16)
        coords = [got[me, 2, k : k + 1, :] - 0.5 for k in range(3)]
        coords = [jnp.broadcast_to(v, (8, TILE)) for v in coords]
        m = jnp.broadcast_to(hot_block[3:4], (8, TILE))
        h = jnp.broadcast_to(hot_block[4:5], (8, TILE))
        pieces(coords, m, h, None, aims, None)
        aim = aims[0].T.astype(jnp.bfloat16)
        for j in range(0, PB // 2, 4):
            total = None
            for u in range(4):
                d = lax.rsqrt(jnp.dot(aim, target[j + u], preferred_element_type=jnp.float32))
                both = d[:, 0:TILE] + d[:, TILE:WIDE]
                total = both if total is None else total + both
            hot_sums[...] += total

    def finish(block, summed):
        return 2.0 * block[3:4, :] / block[4:5, :] - jnp.sum(summed, axis=0, keepdims=True)

    def own_finish(t, carry):
        for half in range(2):
            c = 2 * t + half
            block = dense[c]
            phi = finish(block, sums[t, :, half * TILE : (half + 1) * TILE])
            phis[pl.ds(c, 1), :] = phi
            live = lanes((1, TILE)) + c * TILE < total
            carry = carry + jnp.where(live, block[3:4, :] * phi, 0.0)
        return carry

    carry = lax.fori_loop(0, n_tiles, own_finish, jnp.zeros((1, TILE), jnp.float32))
    energy[...] = jnp.broadcast_to(0.5 * jnp.sum(carry, axis=1, keepdims=True), energy.shape)
    phi = finish(hot_block, hot_sums[...].T)
    share = 0.5 * jnp.sum(hot_block[3:4, :] * phi, axis=1, keepdims=True)
    share = jnp.broadcast_to(share, (1, TILE))
    narrow = lanes((1, TILE))
    eight = rows((8, TILE))
    hot_phi[...] = jnp.where(eight == 0, phi, jnp.where(agreed, least, -1.0))

    for s in range(PB):
        at = offs[s]
        q, r = at // TILE, at % TILE
        both = jnp.where(narrow >= r, phis[pl.ds(q, 1), :], phis[pl.ds(q + 1, 1), :])
        back[s, 0:1, :] = pltpu.roll(both, (TILE - r) % TILE, 1)
        back[s, 1:2, :] = share


def unpack_kernel(place, counts, owners, back, hot_phi, energy_in, result, energy, out):
    me = place[0]
    hot = jnp.max(hot_phi[1:2, :]).astype(jnp.int32)
    lane = lanes((1, TILE))
    out[...] = jnp.zeros(out.shape, jnp.float32)
    special = hot_phi[0:1, :]

    def group(k, carry):
        at, held = carry
        count = counts[0, k]
        q, r = at // TILE, at % TILE
        value = jnp.where(k == hot, special, back[owners[0, k], 0:1, :])
        value = jnp.where(lane < count, value, 0.0)
        rolled = pltpu.roll(value, r, 1)
        merged = jnp.where(lane < r, held, rolled)
        out[pl.ds(q, 1), :] = merged
        out[pl.ds(q + 1, 1), :] = jnp.where(lane < r, rolled, 0.0)
        after = at + count
        held = jnp.where(after // TILE == q, merged, rolled)
        return after, held

    lax.fori_loop(
        0, GROUPS, group, (jnp.int32(0), jnp.zeros((1, TILE), jnp.float32)), unroll=8
    )
    result[...] = out[0:PB, :]
    shares = jnp.sum(back[:, 1, :], axis=0, keepdims=True)
    is_owner = (hot >= 0) & (owners[0, jnp.maximum(hot, 0)] == me)
    energy[...] = jnp.where(is_owner, shares, energy_in[0:1, :])


def per_device(positions, masses, smoothing, block_lists, block_counts, group_owner):
    f32 = jnp.float32
    place = lax.axis_index("slab").astype(jnp.int32).reshape(1)
    lists = block_lists.transpose(0, 2, 1)
    blocks, message = pl.pallas_call(
        pack_kernel,
        out_shape=(
            jax.ShapeDtypeStruct((PB, 8, TILE), f32),
            jax.ShapeDtypeStruct((GROUPS, 3, 4, TILE), f32),
        ),
        in_specs=[SMEM, SMEM, VMEM, VMEM, VMEM],
        out_specs=(VMEM, VMEM),
        compiler_params=params(60),
        name="pack",
    )(
        block_counts,
        group_owner,
        positions.transpose(1, 0, 2).reshape(3, PB, TILE),
        masses.reshape(PB, TILE),
        smoothing.reshape(PB, TILE),
    )
    slabs = lax.axis_size(("slab", "grp"))
    up = [(i, (i + 1) % slabs) for i in range(slabs)]
    down = [(t, s) for s, t in up]
    above = lax.ppermute(blocks, ("slab", "grp"), up)
    got = lax.all_to_all(message, "slab", split_axis=0, concat_axis=0, tiled=True)
    lines = jax.ShapeDtypeStruct((PB, TILE), f32)
    cost = pl.CostEstimate(flops=10**10, bytes_accessed=10**6, transcendentals=0)
    part, upward, sources, targets = pl.pallas_call(
        cross_kernel,
        out_shape=(
            lines,
            lines,
            jax.ShapeDtypeStruct((PB, 32, TILE), jnp.bfloat16),
            jax.ShapeDtypeStruct((PB, 32, 2 * TILE), jnp.bfloat16),
        ),
        in_specs=[pl.BlockSpec(memory_space=pl.ANY), VMEM, VMEM],
        out_specs=(VMEM, VMEM, VMEM, VMEM),
        scratch_shapes=[
            pltpu.VMEM((PB, 16, TILE), jnp.bfloat16),
            pltpu.VMEM((PB, 16, TILE), jnp.bfloat16),
            pltpu.VMEM((PB, 8, TILE), f32),
            pltpu.VMEM((PB, 16, TILE), f32),
            pltpu.VMEM((PB, 16, TILE), f32),
            pltpu.VMEM((PB, 32, TILE), f32),
            pltpu.VMEM((PB, 16, TILE), jnp.bfloat16),
            pltpu.VMEM((PB, 8, TILE), f32),
            pltpu.SMEM((1, COLS, PB), jnp.int32),
            pltpu.SemaphoreType.DMA,
        ],
        compiler_params=params(),
        cost_estimate=cost,
        name="cross",
    )(lists, blocks, above)
    from_below = lax.ppermute(upward, ("slab", "grp"), down)
    back, hot_phi, energy = pl.pallas_call(
        potential_kernel,
        out_shape=(
            jax.ShapeDtypeStruct((GROUPS, 2, TILE), f32),
            jax.ShapeDtypeStruct((8, TILE), f32),
            jax.ShapeDtypeStruct((8, TILE), f32),
        ),
        in_specs=[SMEM, VMEM, pl.BlockSpec(memory_space=pl.ANY)],
        out_specs=(VMEM, VMEM, VMEM),
        scratch_shapes=[
            pltpu.SMEM((PB,), jnp.int32),
            pltpu.VMEM((PB + 8, 8, TILE), f32),
            pltpu.VMEM((PB + 8, TILE), f32),
            pltpu.VMEM((PB // 2, WIDE, 32), jnp.bfloat16),
            pltpu.VMEM((PB // 2 + 1, 32, WIDE), jnp.bfloat16),
            pltpu.VMEM((PB // 2 + 1, 8, WIDE), f32),
            pltpu.VMEM((TILE, TILE), f32),
            pltpu.VMEM((8, 32, TILE), f32),
            pltpu.VMEM((8, 32, TILE), f32),
        ],
        compiler_params=params(),
        cost_estimate=cost,
        name="potential",
    )(place, got, part)
    density = pl.pallas_call(
        rest_kernel,
        out_shape=lines,
        in_specs=[SMEM, VMEM, VMEM, VMEM, VMEM, pl.BlockSpec(memory_space=pl.ANY)],
        out_specs=VMEM,
        scratch_shapes=[pltpu.VMEM((PB, 8, TILE), f32)],
        compiler_params=params(),
        cost_estimate=cost,
        name="rest",
    )(lists, sources, targets, part, from_below, hot_phi)
    returned = lax.all_to_all(back, "slab", split_axis=0, concat_axis=0, tiled=True)
    potential, energy = pl.pallas_call(
        unpack_kernel,
        out_shape=(
            jax.ShapeDtypeStruct((PB, TILE), f32),
            jax.ShapeDtypeStruct((1, TILE), f32),
        ),
        in_specs=[SMEM, SMEM, SMEM, VMEM, VMEM, VMEM],
        out_specs=(VMEM, VMEM),
        scratch_shapes=[pltpu.VMEM((PB + 8, TILE), f32)],
        compiler_params=params(),
        name="unpack",
    )(place, block_counts, group_owner, returned, hot_phi, energy)
    return (
        density.reshape(1, -1),
        potential.reshape(1, -1),
        energy[:, :1],
    )


def solution(mesh):
    placed = (
        P(("slab", "grp"), None, None),
        P(("slab", "grp"), None),
        P(("slab", "grp"), None),
        P(("slab", "grp"), None, None),
        P(("slab", "grp"), None),
        P("grp", None),
    )
    return jax.shard_map(
        per_device,
        mesh=mesh,
        in_specs=placed,
        out_specs=(P(("slab", "grp"), None), P(("slab", "grp"), None), P("grp", "slab")),
        check_vma=False,
    )
```
